32 devices in a mesh: blk: 16 (over z, y, core), dp: 2 (over x).
Axes of the slice: x: 2, y: 2, z: 4, core: 2. Of those that a mesh axis runs over, the one named last changes fastest.
Arguments:
- image_embed: bfloat16 [24576, 1152], P(('dp', 'blk')), parts along dimension 0, may hold values from -6 to 6
- text_embed: bfloat16 [24576, 1152], P(('dp', 'blk')), parts along dimension 0, may hold values from -6 to 6
- logit_scale: float32 [1], replicated, may hold values from 8 to 20
- logit_bias: float32 [1], replicated, may hold values from -1.5 to 0.5
Outputs:
- row_loss: float32 [24576], P(('dp', 'blk')), parts along dimension 0
- grad_image: float32 [24576, 1152], P(('dp', 'blk')), parts along dimension 0
- grad_text: float32 [24576, 1152], P(('dp', 'blk')), parts along dimension 0
The draws below stay inside these ranges and needn't reach their ends.
There are 2 independent parts, one for each index of `dp`. The reference program is written for one: setup_inputs(seed, part) draws one part's arguments, and reference() takes and returns one part's arrays. A program takes and returns all parts, laid end to end along the dimension named above; an argument that names none is the same for every part. Nothing has to cross between parts.
All inputs are finite; a program needn't handle non-finite values.
Results may differ from the reference program's by a relative error of at most 0.0046.
Values may be sent and summed in bfloat16 or wider, within the bound.
A program may use at most 64 MiB of HBM per device.

```python
import math
import jax
import jax.numpy as jnp
from jax import lax

D = 1152
TOK_DEV = 768
TOKENS = 12288
N_BLK = 16


def shard_levels(rng, extent, split, smallest, high):
    def one(axis_at, blocks):
        draws = jax.random.uniform(jax.random.fold_in(jax.random.fold_in(rng, 6), axis_at), (blocks,), jnp.float32, smallest / len(split), high / len(split))
        return jnp.repeat(jnp.exp(draws), extent[axis_at] // blocks).reshape((-1,) + (1,) * (len(extent) - axis_at - 1))

    gain = one(*split[0])
    for cut in split[1:]:
        gain = gain * one(*cut)
    return gain


def scatter_about(own_key, dims, spread, limit, shards=(), held_as=jnp.bfloat16):
    values = spread * jax.random.normal(own_key, dims, jnp.float32)
    if shards:
        values = values * shard_levels(own_key, dims, shards, -0.22, 0.18)
    return jnp.clip(values, -limit, limit).astype(held_as)


def setup_inputs(seed: int = 0, part: int = 0) -> dict:
    splits = jax.random.split(jax.random.key(seed), 5)
    part_keys = jax.random.split(jax.random.fold_in(splits[4], part), 5)
    image_embed = scatter_about(part_keys[0], (TOKENS, D), 1.0, 6.0, ((0, 16),))
    text_embed = scatter_about(part_keys[1], (TOKENS, D), 1.0, 6.0, ((0, 16),))
    logit_scale = jnp.clip(jnp.exp(jax.random.uniform(splits[2], (1,), jnp.float32, math.log(8.0), math.log(20.0))), 8.0, 20.0)
    logit_bias = jnp.clip(jax.random.uniform(splits[3], (1,), jnp.float32, -1.5, 0.5), -1.5, 0.5)
    return dict(image_embed=image_embed, text_embed=text_embed, logit_scale=logit_scale, logit_bias=logit_bias)


EPS = 1e-06

def normalize(x):
    xf = x.astype(jnp.float32)
    inv = lax.rsqrt(lax.optimization_barrier(jnp.sum(xf * xf, axis=-1, keepdims=True)) + EPS)
    return (xf * inv, inv)

def tile_terms(left, right, scale, bias, sign):
    logits = scale * jnp.dot(left, right.T, preferred_element_type=jnp.float32) + bias
    losses = lax.optimization_barrier(jnp.sum(jax.nn.softplus(-sign * logits), axis=1))
    coef = (-scale * sign * jax.nn.sigmoid(-sign * logits)).astype(jnp.bfloat16)
    return (losses, coef)

def unnormalize(unit, inv, grad):
    return inv * (grad - unit * lax.optimization_barrier(jnp.sum(unit * grad, axis=-1, keepdims=True)))

def reference(image_embed, text_embed, logit_scale, logit_bias):
    scale = logit_scale[0]
    bias = logit_bias[0]
    img_unit, inv_img = normalize(image_embed)
    txt_unit, inv_txt = normalize(text_embed)
    img_low = img_unit.astype(jnp.bfloat16)
    txt_low = txt_unit.astype(jnp.bfloat16)
    blocks = N_BLK
    img_blocks = img_low.reshape(blocks, TOK_DEV, D)
    txt_blocks = txt_low.reshape(blocks, TOK_DEV, D)
    rows = jnp.arange(TOK_DEV, dtype=jnp.int32)
    diag_sign = jnp.where(rows[:, None] == rows[None, :], 1.0, -1.0).astype(jnp.float32)

    def per_block(index):
        left = img_blocks[index]
        total_loss = jnp.zeros((TOK_DEV,), jnp.float32)
        g_img = jnp.zeros((TOK_DEV, D), jnp.float32)
        text_terms = []
        for step in range(3):
            right = txt_blocks[(index - step) % blocks]
            sign = diag_sign if step == 0 else jnp.float32(-1.0)
            losses, coef = tile_terms(left, right, scale, bias, sign)
            total_loss = total_loss + losses
            g_img = g_img + jnp.dot(coef, right, preferred_element_type=jnp.float32)
            text_terms.append(jnp.dot(coef.T, left, preferred_element_type=jnp.float32))
        return (total_loss, g_img, text_terms[0], text_terms[1], text_terms[2])
    losses, g_img, term_own, term_one, term_two = lax.map(per_block, jnp.arange(blocks, dtype=jnp.int32))
    g_txt = term_own + jnp.roll(term_one, -1, axis=0) + jnp.roll(term_two, -2, axis=0)
    row_loss = losses.reshape(TOKENS) / (3 * TOK_DEV)
    grad_image = unnormalize(img_unit, inv_img, g_img.reshape(TOKENS, D))
    grad_text = unnormalize(txt_unit, inv_txt, g_txt.reshape(TOKENS, D))
    return (row_loss, grad_image, grad_text)
```

```python
import functools

import jax
import jax.numpy as jnp
from jax import lax
from jax.experimental import pallas as pl
from jax.experimental.pallas import tpu as pltpu
from jax.sharding import PartitionSpec as P

EPS = 1e-06
MESH = pl.DeviceIdType.MESH
TXT, IMG = 0, 1


def normalize(x):
    xf = x.astype(jnp.float32)
    inv = lax.rsqrt(jnp.sum(xf * xf, axis=-1, keepdims=True) + EPS)
    return xf * inv, inv


def dot_t(left, right):
    return lax.dot_general(left, right, (((1,), (1,)), ((), ())), preferred_element_type=jnp.float32)


def dot(left, right):
    return jnp.dot(left, right, preferred_element_type=jnp.float32)


def terms(x):
    e = jnp.exp(-jnp.abs(x))
    loss = jnp.maximum(x, 0.0) + jnp.log1p(e)
    sig = jnp.where(x >= 0.0, 1.0, e) / (1.0 + e)
    return loss, sig


def exchange(n, chunk, scale_ref, bias_ref, img_ref, txt_ref, acc, loss,
             low, far, send_sem, recv_sem):
    rows = img_ref.shape[0]
    count = rows // chunk
    me = lax.axis_index("blk")
    parity = lax.rem(me, 2)

    def at(step):
        return {"blk": lax.rem(me + step + n, n)}

    barrier = pltpu.get_barrier_semaphore()
    for step in (1, -1, 2, -2):
        pl.semaphore_signal(barrier, inc=1, device_id=at(step), device_id_type=MESH)

    def make_low(c):
        here = pl.ds(pl.multiple_of(c * chunk, chunk), chunk)
        low[TXT, here, :] = normalize(txt_ref[here, :])[0].astype(jnp.bfloat16)
        low[IMG, here, :] = normalize(img_ref[here, :])[0].astype(jnp.bfloat16)

    def copies(c):
        here = pl.ds(pl.multiple_of(c * chunk, chunk), chunk)

        def copy(src, kind, dist, slot, to):
            return pltpu.make_async_remote_copy(
                src_ref=src, dst_ref=far.at[kind, dist, here, :],
                send_sem=send_sem.at[slot, c], recv_sem=recv_sem.at[kind, dist, c],
                device_id=to, device_id_type=MESH)

        sign = 1 - 2 * parity
        two = at(2 * sign)
        one = at(sign)
        return (
            copy(low.at[parity, here, :], parity, 1, 2, two),
            copy(low.at[TXT, here, :], TXT, 0, 0, at(1)),
            copy(low.at[IMG, here, :], IMG, 0, 1, at(-1)),
            copy(far.at[parity, 0, here, :], parity, 1, 3, one),
        )

    make_low(0)
    pl.semaphore_wait(barrier, 4)

    def start(c, _):
        direct_two, text_one, image_one, _ = copies(c)
        direct_two.start()
        text_one.start()
        image_one.start()

        @pl.when(c + 1 < count)
        def _():
            make_low(c + 1)
        return 0

    lax.fori_loop(0, count, start, 0)

    scale = scale_ref[0]
    bias = bias_ref[0]
    acc[...] = jnp.zeros_like(acc)
    loss[...] = jnp.zeros_like(loss)

    def own(c, _):
        here = pl.ds(pl.multiple_of(c * chunk, chunk), chunk)
        text = low[TXT, here, :]
        logits = scale * dot_t(low[IMG], text) + bias
        row = lax.broadcasted_iota(jnp.int32, logits.shape, 0)
        col = lax.broadcasted_iota(jnp.int32, logits.shape, 1) + c * chunk
        flip = jnp.where(row == col, -1.0, 1.0).astype(jnp.float32)
        part, sig = terms(flip * logits)
        coef = (scale * flip * sig).astype(jnp.bfloat16)
        loss[IMG] += part
        acc[IMG] += dot(coef, text)
        acc[TXT, here, :] = lax.dot_general(
            coef, low[IMG], (((0,), (0,)), ((), ())), preferred_element_type=jnp.float32)
        return 0

    lax.fori_loop(0, count, own, 0)

    def foreign(kind, dist, c):
        here = pl.ds(pl.multiple_of(c * chunk, chunk), chunk)
        block = far[kind, dist, here, :]
        mine = 1 - kind
        part, sig = terms(scale * dot_t(low[mine], block) + bias)
        loss[mine] += part
        acc[mine] += dot((scale * sig).astype(jnp.bfloat16), block)

    def near(c, _):
        _, text_one, image_one, _ = copies(c)

        @pl.when(parity == 0)
        def _():
            image_one.wait_recv()

        @pl.when(parity == 1)
        def _():
            text_one.wait_recv()
        foreign(1 - parity, 0, c)
        return 0

    lax.fori_loop(0, count, near, 0)

    def across(c, _):
        direct_two, text_one, image_one, relay = copies(c)

        @pl.when(parity == 0)
        def _():
            text_one.wait_recv()

        @pl.when(parity == 1)
        def _():
            image_one.wait_recv()
        relay.start()
        foreign(parity, 0, c)
        direct_two.wait_recv()
        foreign(parity, 1, c)
        here = pl.ds(pl.multiple_of(c * chunk, chunk), chunk)
        pltpu.make_async_remote_copy(
            src_ref=far.at[parity, 0, here, :], dst_ref=far.at[1 - parity, 1, here, :],
            send_sem=send_sem.at[3, c], recv_sem=recv_sem.at[1 - parity, 1, c],
            device_id=at(1), device_id_type=MESH).wait_recv()
        foreign(1 - parity, 1, c)
        return 0

    lax.fori_loop(0, count, across, 0)

    def finish(c, _):
        for copy in copies(c):
            copy.wait_send()
        return 0

    lax.fori_loop(0, count, finish, 0)


def unnormalize(img_ref, txt_ref, acc_ref, loss_ref, img_out, txt_out, row_out):
    for kind, x, out in ((IMG, img_ref, img_out), (TXT, txt_ref, txt_out)):
        unit, inv = normalize(x[...])
        g = acc_ref[kind]
        out[...] = inv * (g - unit * jnp.sum(unit * g, axis=-1, keepdims=True))
    row_out[...] = jnp.sum(loss_ref[...].T, axis=0, keepdims=True)[None]


def shards(n, image_embed, text_embed, logit_scale, logit_bias):
    rows, width = image_embed.shape
    chunk = 128
    count = rows // chunk
    vmem = pl.BlockSpec(memory_space=pltpu.VMEM)
    smem = pl.BlockSpec(memory_space=pltpu.SMEM)
    acc, loss = pl.pallas_call(
        functools.partial(exchange, n, chunk),
        out_shape=(jax.ShapeDtypeStruct((2, rows, width), jnp.float32),
                   jax.ShapeDtypeStruct((2, rows, chunk), jnp.float32)),
        in_specs=[smem, smem, vmem, vmem],
        out_specs=(vmem, vmem),
        scratch_shapes=[
            pltpu.VMEM((2, rows, width), jnp.bfloat16),
            pltpu.VMEM((2, 2, rows, width), jnp.bfloat16),
            pltpu.SemaphoreType.DMA((4, count)),
            pltpu.SemaphoreType.DMA((2, 2, count)),
        ],
        compiler_params=pltpu.CompilerParams(
            collective_id=0, has_side_effects=True, vmem_limit_bytes=48 * 2**20),
        cost_estimate=pl.CostEstimate(
            flops=22 * rows * rows * width, bytes_accessed=12 * rows * width,
            transcendentals=10 * rows * rows),
    )(logit_scale, logit_bias, image_embed, text_embed)
    block = pl.BlockSpec((chunk, width), lambda c: (c, 0))
    grad_image, grad_text, row_loss = pl.pallas_call(
        unnormalize,
        grid=(count,),
        out_shape=(jax.ShapeDtypeStruct((rows, width), jnp.float32),
                   jax.ShapeDtypeStruct((rows, width), jnp.float32),
                   jax.ShapeDtypeStruct((count, 1, chunk), jnp.float32)),
        in_specs=[block, block,
                  pl.BlockSpec((2, chunk, width), lambda c: (0, c, 0)),
                  pl.BlockSpec((None, chunk, chunk), lambda c: (IMG, c, 0))],
        out_specs=(block, block, pl.BlockSpec((1, 1, chunk), lambda c: (c, 0, 0))),
        compiler_params=pltpu.CompilerParams(vmem_limit_bytes=32 * 2**20),
    )(image_embed, text_embed, acc, loss)
    return row_loss.reshape(rows) / (3 * rows), grad_image, grad_text


def solution(mesh):
    in_specs = (P(("dp", "blk"), None), P(("dp", "blk"), None), P(), P())
    out_specs = (P(("dp", "blk")), P(("dp", "blk"), None), P(("dp", "blk"), None))
    return jax.shard_map(functools.partial(shards, mesh.shape["blk"]), mesh=mesh,
                         in_specs=in_specs, out_specs=out_specs, check_vma=False)
```

```python
import functools

import jax
import jax.numpy as jnp
from jax import lax
from jax.experimental import pallas as pl
from jax.experimental.pallas import tpu as pltpu
from jax.sharding import PartitionSpec as P

EPS = 1e-06
MESH = pl.DeviceIdType.MESH
TXT, IMG = 0, 1


def normalize(x):
    xf = x.astype(jnp.float32)
    inv = lax.rsqrt(jnp.sum(xf * xf, axis=-1, keepdims=True) + EPS)
    return xf * inv, inv


def dot_t(left, right):
    return lax.dot_general(left, right, (((1,), (1,)), ((), ())), preferred_element_type=jnp.float32)


def dot(left, right):
    return jnp.dot(left, right, preferred_element_type=jnp.float32)


def terms(x):
    e = jnp.exp(-jnp.abs(x))
    loss = jnp.maximum(x, 0.0) + jnp.log1p(e)
    sig = jnp.where(x >= 0.0, 1.0, e) / (1.0 + e)
    return loss, sig


def exchange(n, chunk, scale_ref, bias_ref, img_hbm, txt_hbm, acc, row_out,
             raw, low, far, inverse, loss, load_sem, send_sem, recv_sem):
    rows = raw.shape[1]
    count = rows // chunk
    me = lax.axis_index("blk")
    parity = lax.rem(me, 2)
    sign = 1 - 2 * parity

    def at(step):
        return {"blk": lax.rem(me + step + n, n)}

    def span(c):
        return pl.ds(pl.multiple_of(c * chunk, chunk), chunk)

    def loads(c):
        return [pltpu.make_async_copy(source.at[span(c), :], raw.at[kind, span(c), :], load_sem.at[kind, c])
                for kind, source in ((TXT, txt_hbm), (IMG, img_hbm))]

    def copy(src, kind, dist, slot, c, to):
        return pltpu.make_async_remote_copy(
            src_ref=src, dst_ref=far.at[kind, dist, span(c), :],
            send_sem=send_sem.at[slot, c], recv_sem=recv_sem.at[kind, dist, c],
            device_id=to, device_id_type=MESH)

    def text_one(c):
        return copy(low.at[TXT, span(c), :], TXT, 0, 0, c, at(1))

    def image_one(c):
        return copy(low.at[IMG, span(c), :], IMG, 0, 1, c, at(-1))

    def direct_two(c):
        return copy(low.at[parity, span(c), :], parity, 1, 2, c, at(2 * sign))

    def relay(c):
        return copy(far.at[parity, 0, span(c), :], parity, 1, 3, c, at(sign))

    def arrived(kind, dist, c):
        copy(far.at[kind, dist, span(c), :], kind, dist, 0, c, at(1)).wait_recv()

    def each(body, low_c=0, high_c=count):
        def step(c, carry):
            body(c)
            return carry
        lax.fori_loop(low_c, high_c, step, 0)

    barrier = pltpu.get_barrier_semaphore()
    for step in (1, -1, 2, -2):
        pl.semaphore_signal(barrier, inc=1, device_id=at(step), device_id_type=MESH)

    @each
    def _(c):
        for load in loads(c):
            load.start()

    def make_low(c):
        for load in loads(c):
            load.wait()
        for kind in (TXT, IMG):
            unit, inv = normalize(raw[kind, span(c), :])
            low[kind, span(c), :] = unit.astype(jnp.bfloat16)
            inverse[kind, span(c), :] = inv

    make_low(0)
    pl.semaphore_wait(barrier, 4)

    @each
    def _(c):
        text_one(c).start()
        image_one(c).start()

        @pl.when(c + 1 < count)
        def _():
            make_low(c + 1)

    scale = scale_ref[0]
    bias = bias_ref[0]
    acc[IMG] = jnp.zeros_like(acc[IMG])
    loss[...] = jnp.zeros_like(loss)

    @each
    def _(c):
        text = low[TXT, span(c), :]
        logits = scale * dot_t(low[IMG], text) + bias
        row = lax.broadcasted_iota(jnp.int32, logits.shape, 0)
        col = lax.broadcasted_iota(jnp.int32, logits.shape, 1) + c * chunk
        flip = jnp.where(row == col, -1.0, 1.0).astype(jnp.float32)
        part, sig = terms(flip * logits)
        coef = (scale * flip * sig).astype(jnp.bfloat16)
        loss[IMG] += part
        acc[IMG] += dot(coef, text)
        acc[TXT, span(c), :] = lax.dot_general(
            coef, low[IMG], (((0,), (0,)), ((), ())), preferred_element_type=jnp.float32)

    def foreign(kind, dist, c):
        block = far[kind, dist, span(c), :]
        mine = 1 - kind
        part, sig = terms(scale * dot_t(low[mine], block) + bias)
        loss[mine] += part
        acc[mine] += dot((scale * sig).astype(jnp.bfloat16), block)

    def take(kind, dist, c):
        arrived(kind, dist, c)
        foreign(kind, dist, c)

    def finish(kind):
        @each
        def _(c):
            inv = inverse[kind, span(c), :]
            unit = raw[kind, span(c), :].astype(jnp.float32) * inv
            g = acc[kind, span(c), :]
            acc[kind, span(c), :] = inv * (g - unit * jnp.sum(unit * g, axis=-1, keepdims=True))

    each(lambda c: take(1 - parity, 0, c))

    each(lambda c: direct_two(c).start())
    lag = count // 2

    @each
    def _(c):
        arrived(parity, 0, c)
        relay(c).start()
        foreign(parity, 0, c)

        @pl.when(c >= lag)
        def _():
            take(parity, 1, c - lag)

    each(lambda c: take(1 - parity, 1, c))
    finish(parity)
    each(lambda c: take(parity, 1, c), count - lag)
    finish(1 - parity)

    @each
    def _(c):
        lanes = jnp.sum(loss[IMG, span(c), :].T, axis=0, keepdims=True)
        row_out[c] = lanes / (3 * rows)

    @each
    def _(c):
        for sent in (text_one, image_one, direct_two, relay):
            sent(c).wait_send()


def shards(n, image_embed, text_embed, logit_scale, logit_bias):
    rows, width = image_embed.shape
    chunk = 128
    count = rows // chunk
    vmem = pl.BlockSpec(memory_space=pltpu.VMEM)
    smem = pl.BlockSpec(memory_space=pltpu.SMEM)
    hbm = pl.BlockSpec(memory_space=pltpu.HBM)
    grads, row_loss = pl.pallas_call(
        functools.partial(exchange, n, chunk),
        out_shape=(jax.ShapeDtypeStruct((2, rows, width), jnp.float32),
                   jax.ShapeDtypeStruct((count, 1, chunk), jnp.float32)),
        in_specs=[smem, smem, hbm, hbm],
        out_specs=(vmem, vmem),
        scratch_shapes=[
            pltpu.VMEM((2, rows, width), jnp.bfloat16),
            pltpu.VMEM((2, rows, width), jnp.bfloat16),
            pltpu.VMEM((2, 2, rows, width), jnp.bfloat16),
            pltpu.VMEM((2, rows, 1), jnp.float32),
            pltpu.VMEM((2, rows, chunk), jnp.float32),
            pltpu.SemaphoreType.DMA((2, count)),
            pltpu.SemaphoreType.DMA((4, count)),
            pltpu.SemaphoreType.DMA((2, 2, count)),
        ],
        compiler_params=pltpu.CompilerParams(
            collective_id=0, has_side_effects=True, vmem_limit_bytes=28 * 2**20),
        cost_estimate=pl.CostEstimate(
            flops=22 * rows * rows * width, bytes_accessed=12 * rows * width,
            transcendentals=10 * rows * rows),
    )(logit_scale, logit_bias, image_embed, text_embed)
    return row_loss.reshape(rows), grads[IMG], grads[TXT]


def solution(mesh):
    in_specs = (P(("dp", "blk"), None), P(("dp", "blk"), None), P(), P())
    out_specs = (P(("dp", "blk")), P(("dp", "blk"), None), P(("dp", "blk"), None))
    return jax.shard_map(functools.partial(shards, mesh.shape["blk"]), mesh=mesh,
                         in_specs=in_specs, out_specs=out_specs, check_vma=False)
```

```python
import functools

import jax
import jax.numpy as jnp
from jax import lax
from jax.experimental import pallas as pl
from jax.experimental.pallas import tpu as pltpu
from jax.sharding import PartitionSpec as P

EPS = 1e-06
MESH = pl.DeviceIdType.MESH
TXT, IMG = 0, 1


def normalize(x):
    xf = x.astype(jnp.float32)
    inv = lax.rsqrt(jnp.sum(xf * xf, axis=-1, keepdims=True) + EPS)
    return xf * inv, inv


def dot_t(left, right):
    return lax.dot_general(left, right, (((1,), (1,)), ((), ())), preferred_element_type=jnp.float32)


def dot(left, right):
    return jnp.dot(left, right, preferred_element_type=jnp.float32)


def sigmoid(x, e):
    return jnp.where(x >= 0.0, 1.0, e) / (1.0 + e)


def softplus(x, e):
    return jnp.maximum(x, 0.0) + jnp.log1p(e)


def exchange(n, chunk, scale_ref, bias_ref, img_hbm, txt_hbm, acc, row_out,
             raw, low, far, inverse, loss, load_sem, send_sem, recv_sem):
    rows = raw.shape[1]
    count = rows // chunk
    me = lax.axis_index("blk")
    parity = lax.rem(me, 2)
    sign = 1 - 2 * parity

    def at(step):
        return {"blk": lax.rem(me + step + n, n)}

    def span(c):
        return pl.ds(pl.multiple_of(c * chunk, chunk), chunk)

    def loads(c):
        return [pltpu.make_async_copy(source.at[span(c), :], raw.at[kind, span(c), :], load_sem.at[kind, c])
                for kind, source in ((TXT, txt_hbm), (IMG, img_hbm))]

    def copy(src, kind, dist, slot, c, to):
        return pltpu.make_async_remote_copy(
            src_ref=src, dst_ref=far.at[kind, dist, span(c), :],
            send_sem=send_sem.at[slot, c], recv_sem=recv_sem.at[kind, dist, c],
            device_id=to, device_id_type=MESH)

    def text_one(c):
        return copy(low.at[TXT, span(c), :], TXT, 0, 0, c, at(1))

    def image_one(c):
        return copy(low.at[IMG, span(c), :], IMG, 0, 1, c, at(-1))

    def direct_two(c):
        return copy(low.at[parity, span(c), :], parity, 1, 2, c, at(2 * sign))

    def relay(c):
        return copy(far.at[parity, 0, span(c), :], parity, 1, 3, c, at(sign))

    def arrived(kind, dist, c):
        copy(far.at[kind, dist, span(c), :], kind, dist, 0, c, at(1)).wait_recv()

    def each(body, low_c=0, high_c=count):
        def step(c, carry):
            body(c)
            return carry
        lax.fori_loop(low_c, high_c, step, 0)

    barrier = pltpu.get_barrier_semaphore()
    for step in (1, -1, 2, -2):
        pl.semaphore_signal(barrier, inc=1, device_id=at(step), device_id_type=MESH)

    @each
    def _(c):
        for load in loads(c):
            load.start()

    def make_low(c):
        for load in loads(c):
            load.wait()
        for kind in (TXT, IMG):
            unit, inv = normalize(raw[kind, span(c), :])
            low[kind, span(c), :] = unit.astype(jnp.bfloat16)
            inverse[kind, span(c), :] = inv

    make_low(0)
    pl.semaphore_wait(barrier, 4)

    @each
    def _(c):
        text_one(c).start()
        image_one(c).start()

        @pl.when(c + 1 < count)
        def _():
            make_low(c + 1)

    scale = scale_ref[0]
    bias = bias_ref[0]
    acc[IMG] = jnp.zeros_like(acc[IMG])
    loss[...] = jnp.zeros_like(loss)

    @each
    def _(c):
        text = low[TXT, span(c), :]
        logits = scale * dot_t(low[IMG], text) + bias
        row = lax.broadcasted_iota(jnp.int32, logits.shape, 0)
        col = lax.broadcasted_iota(jnp.int32, logits.shape, 1) + c * chunk
        flip = jnp.where(row == col, -1.0, 1.0).astype(jnp.float32)
        x = flip * logits
        e = jnp.exp(-jnp.abs(x))
        loss[...] += softplus(x, e)
        coef = (scale * flip * sigmoid(x, e)).astype(jnp.bfloat16)
        acc[IMG] += dot(coef, text)
        acc[TXT, span(c), :] = lax.dot_general(
            coef, low[IMG], (((0,), (0,)), ((), ())), preferred_element_type=jnp.float32)

    each(lambda c: direct_two(c).start())

    def foreign(kind, dist, c):
        block = far[kind, dist, span(c), :]
        mine = 1 - kind
        x = scale * dot_t(low[mine], block) + bias
        e = jnp.exp(-jnp.abs(x))

        @pl.when(kind == TXT)
        def _():
            loss[...] += softplus(x, e)
        acc[mine] += dot((scale * sigmoid(x, e)).astype(jnp.bfloat16), block)

    def take(kind, dist, c):
        arrived(kind, dist, c)
        foreign(kind, dist, c)

    def finish(kind):
        @each
        def _(c):
            inv = inverse[kind, span(c), :]
            unit = raw[kind, span(c), :].astype(jnp.float32) * inv
            g = acc[kind, span(c), :]
            acc[kind, span(c), :] = inv * (g - unit * jnp.sum(unit * g, axis=-1, keepdims=True))

    each(lambda c: take(1 - parity, 0, c))

    lag = count // 2

    @each
    def _(c):
        arrived(parity, 0, c)
        relay(c).start()
        foreign(parity, 0, c)

        @pl.when(c >= lag)
        def _():
            take(parity, 1, c - lag)

    each(lambda c: take(1 - parity, 1, c))
    finish(parity)
    each(lambda c: take(parity, 1, c), count - lag)
    finish(1 - parity)

    @each
    def _(c):
        lanes = jnp.sum(loss[span(c), :].T, axis=0, keepdims=True)
        row_out[c] = lanes / (3 * rows)

    @each
    def _(c):
        for sent in (text_one, image_one, direct_two, relay):
            sent(c).wait_send()


def shards(n, image_embed, text_embed, logit_scale, logit_bias):
    rows, width = image_embed.shape
    chunk = 256
    count = rows // chunk
    vmem = pl.BlockSpec(memory_space=pltpu.VMEM)
    smem = pl.BlockSpec(memory_space=pltpu.SMEM)
    hbm = pl.BlockSpec(memory_space=pltpu.HBM)
    image_embed = pltpu.with_memory_space_constraint(image_embed, pltpu.HBM)
    text_embed = pltpu.with_memory_space_constraint(text_embed, pltpu.HBM)
    grads, row_loss = pl.pallas_call(
        functools.partial(exchange, n, chunk),
        out_shape=(jax.ShapeDtypeStruct((2, rows, width), jnp.float32),
                   jax.ShapeDtypeStruct((count, 1, chunk), jnp.float32)),
        in_specs=[smem, smem, hbm, hbm],
        out_specs=(vmem, vmem),
        scratch_shapes=[
            pltpu.VMEM((2, rows, width), jnp.bfloat16),
            pltpu.VMEM((2, rows, width), jnp.bfloat16),
            pltpu.VMEM((2, 2, rows, width), jnp.bfloat16),
            pltpu.VMEM((2, rows, 1), jnp.float32),
            pltpu.VMEM((rows, chunk), jnp.float32),
            pltpu.SemaphoreType.DMA((2, count)),
            pltpu.SemaphoreType.DMA((4, count)),
            pltpu.SemaphoreType.DMA((2, 2, count)),
        ],
        compiler_params=pltpu.CompilerParams(
            collective_id=0, has_side_effects=True, vmem_limit_bytes=28 * 2**20),
        cost_estimate=pl.CostEstimate(
            flops=22 * rows * rows * width, bytes_accessed=12 * rows * width,
            transcendentals=10 * rows * rows),
    )(logit_scale, logit_bias, image_embed, text_embed)
    return row_loss.reshape(rows), grads[IMG], grads[TXT]


def solution(mesh):
    in_specs = (P(("dp", "blk"), None), P(("dp", "blk"), None), P(), P())
    out_specs = (P(("dp", "blk")), P(("dp", "blk"), None), P(("dp", "blk"), None))
    return jax.shard_map(functools.partial(shards, mesh.shape["blk"]), mesh=mesh,
                         in_specs=in_specs, out_specs=out_specs, check_vma=False)
```

```python
import functools

import jax
import jax.numpy as jnp
from jax import lax
from jax.experimental import pallas as pl
from jax.experimental.pallas import tpu as pltpu
from jax.sharding import PartitionSpec as P

EPS = 1e-06
MESH = pl.DeviceIdType.MESH
TXT, IMG = 0, 1


def normalize(x):
    xf = x.astype(jnp.float32)
    inv = lax.rsqrt(jnp.sum(xf * xf, axis=-1, keepdims=True) + EPS)
    return xf * inv, inv


def dot_t(left, right):
    return lax.dot_general(left, right, (((1,), (1,)), ((), ())), preferred_element_type=jnp.float32)


def dot(left, right):
    return jnp.dot(left, right, preferred_element_type=jnp.float32)


def sigmoid(x, e):
    return jnp.where(x >= 0.0, 1.0, e) / (1.0 + e)


def softplus(x, e):
    return jnp.maximum(x, 0.0) + jnp.log1p(e)


def exchange(n, chunk, scale_ref, bias_ref, img_hbm, txt_hbm, acc, row_out,
             raw, low, far, inverse, loss, load_sem, send_sem, recv_sem):
    rows = raw.shape[1]
    count = rows // chunk
    me = lax.axis_index("blk")
    parity = lax.rem(me, 2)
    sign = 1 - 2 * parity

    def at(step):
        return {"blk": lax.rem(me + step + n, n)}

    def span(c):
        return pl.ds(pl.multiple_of(c * chunk, chunk), chunk)

    def loads(c):
        return [pltpu.make_async_copy(source.at[span(c), :], raw.at[kind, span(c), :], load_sem.at[kind, c])
                for kind, source in ((TXT, txt_hbm), (IMG, img_hbm))]

    def copy(src, kind, dist, slot, c, to):
        return pltpu.make_async_remote_copy(
            src_ref=src, dst_ref=far.at[kind, dist, span(c), :],
            send_sem=send_sem.at[slot, c], recv_sem=recv_sem.at[kind, dist, c],
            device_id=to, device_id_type=MESH)

    def text_one(c):
        return copy(low.at[TXT, span(c), :], TXT, 0, 0, c, at(1))

    def image_one(c):
        return copy(low.at[IMG, span(c), :], IMG, 0, 1, c, at(-1))

    def direct_two(c):
        return copy(low.at[parity, span(c), :], parity, 1, 2, c, at(2 * sign))

    def relay(c):
        return copy(far.at[parity, 0, span(c), :], parity, 1, 3, c, at(sign))

    def arrived(kind, dist, c):
        copy(far.at[kind, dist, span(c), :], kind, dist, 0, c, at(1)).wait_recv()

    def each(body):
        def step(c, carry):
            body(c)
            return carry
        lax.fori_loop(0, count, step, 0)

    barrier = pltpu.get_barrier_semaphore()
    for step in (1, -1, 2, -2):
        pl.semaphore_signal(barrier, inc=1, device_id=at(step), device_id_type=MESH)

    @each
    def _(c):
        for load in loads(c):
            load.start()

    def make_low(c):
        for load in loads(c):
            load.wait()
        for kind in (TXT, IMG):
            unit, inv = normalize(raw[kind, span(c), :])
            low[kind, span(c), :] = unit.astype(jnp.bfloat16)
            inverse[kind, span(c), :] = inv

    make_low(0)
    pl.semaphore_wait(barrier, 4)

    @each
    def _(c):
        text_one(c).start()
        image_one(c).start()
        direct_two(c).start()

        @pl.when(c + 1 < count)
        def _():
            make_low(c + 1)

    scale = scale_ref[0]
    bias = bias_ref[0]
    acc[IMG] = jnp.zeros_like(acc[IMG])
    loss[...] = jnp.zeros_like(loss)

    @each
    def _(c):
        text = low[TXT, span(c), :]
        logits = scale * dot_t(low[IMG], text) + bias
        row = lax.broadcasted_iota(jnp.int32, logits.shape, 0)
        col = lax.broadcasted_iota(jnp.int32, logits.shape, 1) + c * chunk
        flip = jnp.where(row == col, -1.0, 1.0).astype(jnp.float32)
        x = flip * logits
        e = jnp.exp(-jnp.abs(x))
        loss[...] += softplus(x, e)
        coef = (scale * flip * sigmoid(x, e)).astype(jnp.bfloat16)
        acc[IMG] += dot(coef, text)
        acc[TXT, span(c), :] = lax.dot_general(
            coef, low[IMG], (((0,), (0,)), ((), ())), preferred_element_type=jnp.float32)

    def foreign(kind, dist, c):
        block = far[kind, dist, span(c), :]
        mine = 1 - kind
        x = scale * dot_t(low[mine], block) + bias
        e = jnp.exp(-jnp.abs(x))

        @pl.when(kind == TXT)
        def _():
            loss[...] += softplus(x, e)
        acc[mine] += dot((scale * sigmoid(x, e)).astype(jnp.bfloat16), block)

    def take(kind, dist, c):
        arrived(kind, dist, c)
        foreign(kind, dist, c)

    def finish(kind):
        @each
        def _(c):
            inv = inverse[kind, span(c), :]
            unit = raw[kind, span(c), :].astype(jnp.float32) * inv
            g = acc[kind, span(c), :]
            acc[kind, span(c), :] = inv * (g - unit * jnp.sum(unit * g, axis=-1, keepdims=True))

    each(lambda c: take(1 - parity, 0, c))

    @each
    def _(c):
        arrived(parity, 0, c)
        relay(c).start()
        foreign(parity, 0, c)

        @pl.when(c >= 1)
        def _():
            take(parity, 1, c - 1)
            take(1 - parity, 1, c - 1)

    last = count - 1
    take(parity, 1, last)
    finish(1 - parity)
    take(1 - parity, 1, last)
    finish(parity)

    @each
    def _(c):
        lanes = jnp.sum(loss[span(c), :].T, axis=0, keepdims=True)
        row_out[c] = lanes / (3 * rows)

    @each
    def _(c):
        for sent in (text_one, image_one, direct_two, relay):
            sent(c).wait_send()


def shards(n, image_embed, text_embed, logit_scale, logit_bias):
    rows, width = image_embed.shape
    chunk = 128
    count = rows // chunk
    vmem = pl.BlockSpec(memory_space=pltpu.VMEM)
    smem = pl.BlockSpec(memory_space=pltpu.SMEM)
    hbm = pl.BlockSpec(memory_space=pltpu.HBM)
    image_embed = pltpu.with_memory_space_constraint(image_embed, pltpu.HBM)
    text_embed = pltpu.with_memory_space_constraint(text_embed, pltpu.HBM)
    grads, row_loss = pl.pallas_call(
        functools.partial(exchange, n, chunk),
        out_shape=(jax.ShapeDtypeStruct((2, rows, width), jnp.float32),
                   jax.ShapeDtypeStruct((count, 1, chunk), jnp.float32)),
        in_specs=[smem, smem, hbm, hbm],
        out_specs=(vmem, vmem),
        scratch_shapes=[
            pltpu.VMEM((2, rows, width), jnp.bfloat16),
            pltpu.VMEM((2, rows, width), jnp.bfloat16),
            pltpu.VMEM((2, 2, rows, width), jnp.bfloat16),
            pltpu.VMEM((2, rows, 1), jnp.float32),
            pltpu.VMEM((rows, chunk), jnp.float32),
            pltpu.SemaphoreType.DMA((2, count)),
            pltpu.SemaphoreType.DMA((4, count)),
            pltpu.SemaphoreType.DMA((2, 2, count)),
        ],
        compiler_params=pltpu.CompilerParams(
            collective_id=0, has_side_effects=True, vmem_limit_bytes=28 * 2**20),
        cost_estimate=pl.CostEstimate(
            flops=22 * rows * rows * width, bytes_accessed=12 * rows * width,
            transcendentals=10 * rows * rows),
    )(logit_scale, logit_bias, image_embed, text_embed)
    return row_loss.reshape(rows), grads[IMG], grads[TXT]


def solution(mesh):
    in_specs = (P(("dp", "blk"), None), P(("dp", "blk"), None), P(), P())
    out_specs = (P(("dp", "blk")), P(("dp", "blk"), None), P(("dp", "blk"), None))
    return jax.shard_map(functools.partial(shards, mesh.shape["blk"]), mesh=mesh,
                         in_specs=in_specs, out_specs=out_specs, check_vma=False)
```
